32 devices in a mesh: head: 2 (over x), ctx: 16 (over z, y, core).
Axes of the slice: x: 2, y: 2, z: 4, core: 2. Of those that a mesh axis runs over, the one named last changes fastest.
Arguments:
- queries: bfloat16 [16384, 2048], P('ctx', 'head'), may hold values from -6 to 6
- key_vectors: bfloat16 [16384, 2048], P('ctx', 'head'), may hold values from -6 to 6
- value_vectors: bfloat16 [16384, 2048], P('ctx', 'head'), may hold values from -6 to 6
- out_grad: bfloat16 [16384, 2048], P('ctx', 'head'), may hold values from -6 to 6
- segment_ids: int32 [16384], P('ctx'), may hold values from 0 to 7, never falling along the last dimension, each value on 1 to 4096 neighbouring positions
- head_gain: float32 [16], P('head'), may hold values from 0.3 to 3
Outputs:
- attended: bfloat16 [16384, 2048], P('ctx', 'head')
- grad_queries: bfloat16 [16384, 2048], P('ctx', 'head')
- grad_keys: bfloat16 [16384, 2048], P('ctx', 'head')
- grad_values: bfloat16 [16384, 2048], P('ctx', 'head')
The draws below stay inside these ranges and needn't reach their ends.
Inputs may be any that keep to these rules, and one draw needn't show every extreme that they name: `segment_ids`: document numbers never fall along the sequence; every document covers 1 to 4096 positions and one covers exactly 4096.
All inputs are finite; a program needn't handle non-finite values.
Results may differ from the reference program's by a relative error of at most 0.0058.
Values sent between devices are 32-bit elements; how exact they have to be, the bound alone decides.
A program may use at most 128 MiB of HBM per device.

```python
import math
import jax
import jax.numpy as jnp
import numpy as np
from jax import lax

HEADS = 16
HS = 128
TOK_DEV = 1024
TOKENS = 16384
DOCS = 8
N_CTX = 16


def levels(rng, extent, shards, least, high):
    level = 1.0
    for dim, parts in shards:
        steps = jax.random.uniform(jax.random.fold_in(jax.random.fold_in(rng, 6), dim), (parts,), jnp.float32, least / len(shards), high / len(shards))
        level = level * jnp.repeat(jnp.exp(steps), extent[dim] // parts).reshape((-1,) + (1,) * (len(extent) - 1 - dim))
    return level


def length_profile(count, total, reach, skew):
    weights = [(1 << 20) // math.isqrt(standing ** skew) + 1 for standing in range(2, count + 1)]
    surplus, holding = total - reach - (count - 1), [1] * (count - 1)
    while surplus > 0:
        movable = [i for i in range(count - 1) if holding[i] < reach]
        pool, remaining = sum([weights[i] for i in movable]), surplus
        for i in movable:
            more = min(reach - holding[i], max(1, remaining * weights[i] // pool), surplus)
            holding[i] = holding[i] + more
            surplus = surplus - more
    return np.array([reach] + holding)


def uneven(stream_key, count, total, most, lean):
    if count == 2:
        one = jax.random.randint(stream_key, (), max(1, total - most), min(most, total - 1) + 1)
        return jnp.stack([one, total - one])
    tallies = jnp.asarray(length_profile(count, total, most, lean), jnp.int32)
    twos = (count - 1) // 2
    donor, taker = tallies[1:1 + 2 * twos:2], tallies[2:2 + 2 * twos:2]
    slack = jnp.minimum(donor - 1, most - taker)
    passed = jax.random.randint(jax.random.fold_in(stream_key, 1), (twos,), 0, 1 << 20) % (slack + 1)
    tallies = tallies.at[1:1 + 2 * twos:2].set(donor - passed).at[2:2 + 2 * twos:2].set(taker + passed)
    return tallies[jax.random.permutation(jax.random.fold_in(stream_key, 2), count)]


def noise(own_key, extent, deviation, most, split=(), dtype=jnp.bfloat16):
    values = deviation * jax.random.normal(own_key, extent, jnp.float32)
    if split:
        values = values * levels(own_key, extent, split, -0.22, 0.18)
    return jnp.clip(values, -most, most).astype(dtype)


def setup_inputs(seed: int = 0) -> dict:
    streams_of = jax.random.split(jax.random.key(seed), 7)
    queries = noise(streams_of[0], (TOKENS, HEADS * HS), 1.0, 6.0, ((0, 16), (1, 2)))
    key_vectors = noise(streams_of[1], (TOKENS, HEADS * HS), 1.0, 6.0, ((0, 16), (1, 2)))
    value_vectors = noise(streams_of[2], (TOKENS, HEADS * HS), 1.0, 6.0, ((0, 16), (1, 2)))
    out_grad = noise(streams_of[3], (TOKENS, HEADS * HS), 1.0, 6.0, ((0, 16), (1, 2)))
    segment_ids = jnp.searchsorted(jnp.cumsum(uneven(streams_of[4], DOCS, TOKENS, TOKENS // 4, 2)), jnp.arange(TOKENS), side="right").astype(jnp.int32)
    head_gain = jnp.clip(jnp.exp(math.log(3.0) - 2.3025851 * jax.random.uniform(streams_of[5], (HEADS,), jnp.float32) ** levels(streams_of[5], (HEADS,), ((0, 2),), -0.2, 0.2)), 0.3, 3.0)
    return {"queries": queries, "key_vectors": key_vectors, "value_vectors": value_vectors, "out_grad": out_grad, "segment_ids": segment_ids, "head_gain": head_gain}


EPS = 1e-05

def allowed_pairs(segments):
    position = jnp.arange(segments.shape[0])
    return (position[:, None] >= position[None, :]) & (segments[:, None] == segments[None, :])

def reference(queries, key_vectors, value_vectors, out_grad, segment_ids, head_gain):
    width = HEADS * HS

    def blocks(array):
        return array.reshape(N_CTX, TOK_DEV, HEADS, HS)
    query_blocks = blocks(queries)
    key_blocks = blocks(key_vectors)
    value_blocks = blocks(value_vectors)
    grad_blocks = blocks(out_grad)
    segment_blocks = segment_ids.reshape(N_CTX, TOK_DEV)
    gain = head_gain.astype(jnp.float32)[None, :, None]
    blank = jnp.zeros((HEADS, HS, HS), jnp.float32)
    start_id = jnp.array(-1, jnp.int32)

    def forward(carry, item):
        prev_close, running = carry
        query_rows, key_rows, value_rows, grad_rows, segments = item
        query_f = query_rows.astype(jnp.float32)
        key_f = key_rows.astype(jnp.float32)
        value_f = value_rows.astype(jnp.float32)
        opening_id = segments[0]
        closing_id = segments[-1]
        allowed = allowed_pairs(segments)[None]
        scores = jnp.einsum('thd,shd->hts', query_f, key_f)
        probs = jnp.where(allowed, scores, 0.0).astype(jnp.bfloat16)
        state_in = jnp.where(prev_close == opening_id, running, 0.0).astype(jnp.bfloat16)
        state_f = state_in.astype(jnp.float32)
        at_open = (segments == opening_id)[:, None, None]
        at_close = (segments == closing_id)[:, None, None]
        attn = jnp.einsum('hts,shd->thd', probs.astype(jnp.float32), value_f)
        attn = attn + jnp.where(at_open, jnp.einsum('thd,hde->the', query_f, state_f), 0.0)
        scaled = attn * gain
        grad_f = grad_rows.astype(jnp.float32)
        power = lax.optimization_barrier(jnp.sum(scaled * scaled, axis=(1, 2)))[:, None, None]
        cross = lax.optimization_barrier(jnp.sum(grad_f * scaled, axis=(1, 2)))[:, None, None]
        scale = lax.rsqrt(power / width + EPS)
        attended = (scaled * scale).astype(jnp.bfloat16)
        inner = (gain * (grad_f * scale - scaled * cross * scale * scale * scale / width)).astype(jnp.bfloat16)
        inner_f = inner.astype(jnp.float32)
        dscores = jnp.einsum('the,she->hts', inner_f, value_f)
        dprobs = jnp.where(allowed, dscores, 0.0).astype(jnp.bfloat16)
        grad_q = jnp.einsum('hts,shd->thd', dprobs.astype(jnp.float32), key_f)
        grad_q = grad_q + jnp.where(at_open, jnp.einsum('the,hde->thd', inner_f, state_f), 0.0)
        tail = jnp.einsum('shd,she->hde', jnp.where(at_close, key_f, 0.0), value_f)
        joined = (prev_close == opening_id) & (opening_id == closing_id)
        running = jnp.where(joined, running + tail, tail)
        back_tail = jnp.einsum('thd,the->hde', jnp.where(at_open, query_f, 0.0), inner_f)
        return ((closing_id, running), (attended, grad_q.astype(jnp.bfloat16), inner, back_tail))
    _, (attended, grad_q, inner, back_tails) = lax.scan(forward, (start_id, blank), (query_blocks, key_blocks, value_blocks, grad_blocks, segment_blocks))

    def backward(carry, item):
        next_open, running = carry
        query_rows, key_rows, value_rows, inner_rows, segments, back_tail = item
        query_f = query_rows.astype(jnp.float32)
        key_f = key_rows.astype(jnp.float32)
        value_f = value_rows.astype(jnp.float32)
        inner_f = inner_rows.astype(jnp.float32)
        opening_id = segments[0]
        closing_id = segments[-1]
        allowed = allowed_pairs(segments)[None]
        scores = jnp.einsum('thd,shd->hts', query_f, key_f)
        probs = jnp.where(allowed, scores, 0.0).astype(jnp.bfloat16).astype(jnp.float32)
        dscores = jnp.einsum('the,she->hts', inner_f, value_f)
        dprobs = jnp.where(allowed, dscores, 0.0).astype(jnp.bfloat16).astype(jnp.float32)
        state_grad = jnp.where(next_open == closing_id, running, 0.0).astype(jnp.bfloat16).astype(jnp.float32)
        at_close = (segments == closing_id)[:, None, None]
        grad_k = jnp.einsum('hts,thd->shd', dprobs, query_f)
        grad_k = grad_k + jnp.where(at_close, jnp.einsum('hde,she->shd', state_grad, value_f), 0.0)
        grad_v = jnp.einsum('hts,the->she', probs, inner_f)
        grad_v = grad_v + jnp.where(at_close, jnp.einsum('hde,shd->she', state_grad, key_f), 0.0)
        joined = (next_open == closing_id) & (opening_id == closing_id)
        running = jnp.where(joined, running + back_tail, back_tail)
        return ((opening_id, running), (grad_k.astype(jnp.bfloat16), grad_v.astype(jnp.bfloat16)))
    _, (grad_k, grad_v) = lax.scan(backward, (start_id, blank), (query_blocks, key_blocks, value_blocks, inner, segment_blocks, back_tails), reverse=True)

    def whole(array):
        return array.reshape(TOKENS, HEADS * HS)
    return (whole(attended), whole(grad_q), whole(grad_k), whole(grad_v))
```

```python
import functools

import jax
import jax.numpy as jnp
from jax import lax
from jax.experimental import pallas as pl
from jax.experimental.pallas import tpu as pltpu
from jax.sharding import PartitionSpec as P

HS = 128
EPS = 1e-05
CHUNK = 256
BF = jnp.bfloat16
F32 = jnp.float32


def dot(a, b, da, db):
    return lax.dot_general(a, b, (((da,), (db,)), ((), ())), preferred_element_type=F32)


def kernel(
    heads, blocks, head_devs, reach,
    q_hbm, k_hbm, v_hbm, g_hbm, seg_ref, gain_ref,
    att_hbm, gq_hbm, gk_hbm, gv_hbm,
    q, k, v, g, att, gq, gk, gv,
    scaled, inner, gkl, gvl, probs, masks, segc,
    use_f, use_b, in_chunk_close, in_chunk_open, in_open, in_close,
    rr, xc, accp, accx, states, ustates, state_in, state_grad,
    tail_f, got_f, comb_f, far_f, back_f, home_f,
    tail_b, got_b, comb_b, far_b, back_b, home_b,
    pc_send, pc_recv,
    load_sem, store_sem, pair_send, pair_recv, far_send, far_recv, pc_ssem, pc_rsem,
):
    rows = q.shape[0]
    chunks = rows // CHUNK
    half = heads // 2
    hr = half * HS
    pairs = blocks // 2
    me = lax.axis_index("ctx")
    hd = lax.axis_index("head")
    pair = me // 2
    core = me % 2
    partner = pair * 2 + 1 - core

    loads = [
        pltpu.make_async_copy(s, d, load_sem.at[i])
        for i, (s, d) in enumerate(((k_hbm, k), (v_hbm, v), (q_hbm, q), (g_hbm, g)))
    ]
    for cp in loads:
        cp.start()

    barrier = pltpu.get_barrier_semaphore()
    pl.semaphore_signal(barrier, inc=1, device_id={"ctx": partner}, device_id_type=pl.DeviceIdType.MESH)
    count = jnp.int32(1)
    for r in range(1, reach + 1):
        for sign in (1, -1):
            other = pair + sign * r
            ok = (other >= 0) & (other < pairs)
            count = count + ok.astype(jnp.int32)

            @pl.when(ok)
            def _(other=other):
                pl.semaphore_signal(
                    barrier, inc=1, device_id={"ctx": other * 2 + core}, device_id_type=pl.DeviceIdType.MESH
                )
    for d in range(1, head_devs):
        pl.semaphore_signal(
            barrier, inc=1, device_id={"head": (hd + d) % head_devs}, device_id_type=pl.DeviceIdType.MESH
        )
        count = count + 1

    seg_row = seg_ref[...].astype(F32)
    segc[...] = jnp.broadcast_to(seg_row, (HS, rows)).T
    opens = [segc[pl.ds(j * CHUNK, 1), :] for j in range(chunks)]
    closes = [segc[pl.ds(j * CHUNK + CHUNK - 1, 1), :] for j in range(chunks)]
    own_open, own_close = opens[0], closes[-1]

    def same(a, b):
        return jnp.where(a == b, 1.0, 0.0)

    causal = lax.broadcasted_iota(jnp.int32, (CHUNK, CHUNK), 0) >= lax.broadcasted_iota(
        jnp.int32, (CHUNK, CHUNK), 1
    )
    for j in range(chunks):
        at = pl.ds(j * CHUNK, CHUNK)
        s = segc[at, :]
        in_chunk_close[at, :] = same(s, closes[j]).astype(BF)
        in_chunk_open[at, :] = same(s, opens[j]).astype(BF)
        in_open[at, :] = same(s, own_open).astype(BF)
        in_close[at, :] = same(s, own_close).astype(BF)
        use_f[at, :] = same(s, closes[max(j - 1, 0)]).astype(BF)
        use_b[at, :] = same(s, opens[min(j + 1, chunks - 1)]).astype(BF)
        wide = jnp.concatenate([s] * (CHUNK // HS), axis=1)
        row = seg_ref[:, j * CHUNK : (j + 1) * CHUNK].astype(F32)
        masks[j] = jnp.where(causal & (wide == row), 1.0, 0.0)
    pass_f = [None] + [same(closes[j], closes[j - 1]) for j in range(1, chunks)]
    pass_b = [same(opens[j], opens[j + 1]) for j in range(chunks - 1)] + [None]

    line = lax.broadcasted_iota(jnp.int32, (8, HS), 0)
    marks = jnp.where(line == 0, own_open, own_close)
    for share in range(2):
        tail_f[share, pl.ds(hr, 8), :] = marks
        tail_b[share, pl.ds(hr, 8), :] = marks

    def cols(h):
        return pl.ds(pl.multiple_of(h * HS, HS), HS)

    def each_head(start, stop, body):
        def turn(h, _):
            body(h, cols(h))
            return 0

        lax.fori_loop(start, stop, turn, 0)

    class Exchange:
        def __init__(self, way, tail, got, comb, far, back, home, result):
            self.way, self.base = way, 0 if way > 0 else 1
            self.tail, self.got, self.comb, self.far = tail, got, comb, far
            self.back, self.home, self.result = back, home, result
            self.first = core == (0 if way > 0 else 1)
            i = self.base * 2
            self.out = pltpu.make_async_remote_copy(
                src_ref=tail.at[1 - core], dst_ref=got,
                send_sem=pair_send.at[i], recv_sem=pair_recv.at[i],
                device_id={"ctx": partner}, device_id_type=pl.DeviceIdType.MESH,
            )
            self.ret = pltpu.make_async_remote_copy(
                src_ref=back, dst_ref=home,
                send_sem=pair_send.at[i + 1], recv_sem=pair_recv.at[i + 1],
                device_id={"ctx": partner}, device_id_type=pl.DeviceIdType.MESH,
            )

        def hop(self, r):
            i = self.base * reach + r - 1
            return pltpu.make_async_remote_copy(
                src_ref=self.comb, dst_ref=self.far.at[r - 1],
                send_sem=far_send.at[i], recv_sem=far_recv.at[i],
                device_id={"ctx": (pair + self.way * r) * 2 + core},
                device_id_type=pl.DeviceIdType.MESH,
            )

        def inside(self, r):
            other = pair + r
            return (other >= 0) & (other < pairs)

        def both(self):
            other_open = self.got[pl.ds(hr, 1), :]
            other_close = self.got[pl.ds(hr + 1, 1), :]
            if self.way > 0:
                own, oth = (own_close, own_open), (other_close, other_open)
            else:
                own, oth = (own_open, own_close), (other_open, other_close)
            pick = [(jnp.where(self.first, a, b), jnp.where(self.first, b, a)) for a, b in zip(own, oth)]
            return pick

        def middle(self):
            self.out.wait()
            (tag_first, tag_last), _ = self.both()
            joined = tag_first == tag_last

            def turn(e, _):
                at = pl.ds(pl.multiple_of(e * HS, HS), HS)
                mine, other = self.tail[core, at, :], self.got[at, :]
                t_first = jnp.where(self.first, mine, other)
                t_last = jnp.where(self.first, other, mine)
                self.comb[at, :] = t_last + jnp.where(joined, t_first, 0.0)
                return 0

            lax.fori_loop(0, half, turn, 0)
            self.comb[pl.ds(hr, 8), :] = jnp.broadcast_to(tag_last, (8, HS))
            for r in range(1, reach + 1):

                @pl.when(self.inside(self.way * r))
                def _(r=r):
                    self.hop(r).start()

                @pl.when(jnp.logical_not(self.inside(-self.way * r)))
                def _(r=r):
                    self.far[r - 1] = jnp.full((hr + 8, HS), -1.0, F32)

        def near(self):
            for r in range(1, reach + 1):

                @pl.when(self.inside(-self.way * r))
                def _(r=r):
                    self.hop(r).wait_recv()

            (tag_first, _), (need_first, need_last) = self.both()
            tags = [self.far[r, pl.ds(hr, 1), :] for r in range(reach)]

            def turn(e, _):
                at = pl.ds(pl.multiple_of(e * HS, HS), HS)
                t_first = jnp.where(self.first, self.tail[core, at, :], self.got[at, :])
                x_first = jnp.zeros((HS, HS), F32)
                x_last = jnp.where(tag_first == need_last, t_first, 0.0)
                for r in range(reach):
                    c = self.far[r, at, :]
                    x_first = x_first + jnp.where(tags[r] == need_first, c, 0.0)
                    x_last = x_last + jnp.where(tags[r] == need_last, c, 0.0)
                self.back[at, :] = jnp.where(self.first, x_last, x_first)
                self.result[core * half + e] = jnp.where(self.first, x_first, x_last).astype(BF)
                return 0

            lax.fori_loop(0, half, turn, 0)
            self.ret.start()

        def finish(self):
            self.ret.wait()

            def turn(e, _):
                at = pl.ds(pl.multiple_of(e * HS, HS), HS)
                self.result[(1 - core) * half + e] = self.home[at, :].astype(BF)
                return 0

            lax.fori_loop(0, half, turn, 0)
            for r in range(1, reach + 1):

                @pl.when(self.inside(self.way * r))
                def _(r=r):
                    self.hop(r).wait_send()

    fwd = Exchange(1, tail_f, got_f, comb_f, far_f, back_f, home_f, state_in)
    bwd = Exchange(-1, tail_b, got_b, comb_b, far_b, back_b, home_b, state_grad)

    loads[0].wait()
    loads[1].wait()

    def tails(h, c):
        s = None
        for j in range(chunks):
            at = pl.ds(j * CHUNK, CHUNK)
            t = dot(k[at, c] * in_chunk_close[at, :], v[at, c], 0, 0)
            s = t if j == 0 else s * pass_f[j] + t
            if j < chunks - 1:
                states[h, j] = s.astype(BF)
        tail_f[h // half, pl.ds(pl.multiple_of((h % half) * HS, HS), HS), :] = s

    each_head(0, heads, tails)
    pl.semaphore_wait(barrier, count)
    fwd.out.start()
    loads[2].wait()

    def local(h, c):
        for j in range(chunks):
            at = pl.ds(j * CHUNK, CHUNK)
            qj = q[at, c]
            p = (dot(qj, k[at, c], 1, 1) * masks[j]).astype(BF)
            probs[h, j] = p
            o = dot(p, v[at, c], 1, 0)
            if j > 0:
                o = o + dot(qj * use_f[at, :], states[h, j - 1], 1, 0)
            scaled[at, c] = o

    early = max(1, heads // 4)
    each_head(0, early, local)
    fwd.middle()
    each_head(early, heads, local)
    loads[3].wait()
    fwd.near()
    accp[...] = jnp.zeros_like(accp)
    accx[...] = jnp.zeros_like(accx)
    fwd.finish()

    def norm(h, c):
        gain = gain_ref[h]
        for j in range(chunks):
            at = pl.ds(j * CHUNK, CHUNK)
            a = scaled[at, c] + dot(q[at, c] * in_open[at, :], state_in[h], 1, 0)
            a = a * gain
            scaled[at, c] = a
            accp[at, :] += a * a
            accx[at, :] += a * g[at, c].astype(F32)

    each_head(0, heads, norm)

    pc_send[pl.ds(0, 1), :] = jnp.sum(accp[...].T, axis=0, keepdims=True)
    pc_send[pl.ds(1, 1), :] = jnp.sum(accx[...].T, axis=0, keepdims=True)
    pc_send[pl.ds(2, 6), :] = jnp.zeros((6, rows), F32)
    swaps = [
        pltpu.make_async_remote_copy(
            src_ref=pc_send, dst_ref=pc_recv.at[d - 1],
            send_sem=pc_ssem.at[d - 1], recv_sem=pc_rsem.at[d - 1],
            device_id={"head": (hd + d) % head_devs}, device_id_type=pl.DeviceIdType.MESH,
        )
        for d in range(1, head_devs)
    ]
    for cp in swaps:
        cp.start()
    for cp in swaps:
        cp.wait()
    power, cross = pc_send[pl.ds(0, 1), :], pc_send[pl.ds(1, 1), :]
    for d in range(head_devs - 1):
        power = power + pc_recv[d, pl.ds(0, 1), :]
        cross = cross + pc_recv[d, pl.ds(1, 1), :]
    width = head_devs * heads * HS
    r = lax.rsqrt(power / width + EPS)
    rr[...] = jnp.broadcast_to(r, (HS, rows)).T
    xc[...] = jnp.broadcast_to(cross * r * r * r / width, (HS, rows)).T

    def inners(h, c):
        gain = gain_ref[h]
        u = None
        for j in reversed(range(chunks)):
            at = pl.ds(j * CHUNK, CHUNK)
            a, rj = scaled[at, c], rr[at, :]
            att[at, c] = (a * rj).astype(BF)
            i = (gain * (g[at, c].astype(F32) * rj - a * xc[at, :])).astype(BF)
            inner[at, c] = i
            b = dot(q[at, c] * in_chunk_open[at, :], i, 0, 0)
            u = b if j == chunks - 1 else u * pass_b[j] + b
            if j > 0:
                ustates[h, j - 1] = u.astype(BF)
        tail_b[h // half, pl.ds(pl.multiple_of((h % half) * HS, HS), HS), :] = u

    each_head(0, heads, inners)
    bwd.out.start()
    stores = [
        pltpu.make_async_copy(s, d, store_sem.at[i])
        for i, (s, d) in enumerate(((att, att_hbm), (gq, gq_hbm), (gk, gk_hbm), (gv, gv_hbm)))
    ]
    stores[0].start()

    def grads(h, c):
        for j in range(chunks):
            at = pl.ds(j * CHUNK, CHUNK)
            i, kj, vj = inner[at, c], k[at, c], v[at, c]
            d = (dot(i, vj, 1, 1) * masks[j]).astype(BF)
            a = dot(d, kj, 1, 0) + dot(i * in_open[at, :], state_in[h], 1, 1)
            if j > 0:
                a = a + dot(i * use_f[at, :], states[h, j - 1], 1, 1)
            gq[at, c] = a.astype(BF)
            b = dot(d, q[at, c], 0, 0)
            e = dot(probs[h, j], i, 0, 0)
            if j < chunks - 1:
                b = b + dot(vj * use_b[at, :], ustates[h, j], 1, 1)
                e = e + dot(kj * use_b[at, :], ustates[h, j], 1, 0)
            gkl[at, c] = b
            gvl[at, c] = e

    each_head(0, early, grads)
    bwd.middle()
    each_head(early, heads, grads)
    stores[1].start()
    bwd.near()
    bwd.finish()

    def last(h, c):
        for j in range(chunks):
            at = pl.ds(j * CHUNK, CHUNK)
            m = in_close[at, :]
            gk[at, c] = (gkl[at, c] + dot(v[at, c] * m, state_grad[h], 1, 1)).astype(BF)
            gv[at, c] = (gvl[at, c] + dot(k[at, c] * m, state_grad[h], 1, 0)).astype(BF)

    each_head(0, heads, last)
    stores[2].start()
    stores[3].start()
    for cp in stores:
        cp.wait()


def per_device(queries, key_vectors, value_vectors, out_grad, segment_ids, head_gain):
    rows, width = queries.shape
    heads = head_gain.shape[0]
    blocks = lax.axis_size("ctx")
    head_devs = lax.axis_size("head")
    reach = max(1, (blocks // 4 + 1) // 2)
    chunks = rows // CHUNK
    hr = heads // 2 * HS
    V = pltpu.VMEM
    whole = V((rows, width), BF)
    lanes = V((rows, HS), BF)
    flanes = V((rows, HS), F32)
    msg = V((hr + 8, HS), F32)
    comm = [V((2, hr + 8, HS), F32), msg, msg, V((reach, hr + 8, HS), F32), V((hr, HS), F32), V((hr, HS), F32)]
    peers = max(1, head_devs - 1)
    dma = pltpu.SemaphoreType.DMA
    scratch = (
        [whole] * 8
        + [V((rows, width), F32), whole, V((rows, width), F32), V((rows, width), F32)]
        + [V((heads, chunks, CHUNK, CHUNK), BF), V((chunks, CHUNK, CHUNK), F32), flanes]
        + [lanes] * 6
        + [flanes] * 4
        + [V((heads, chunks - 1, HS, HS), BF)] * 2
        + [V((heads, HS, HS), BF)] * 2
        + comm
        + comm
        + [V((8, rows), F32), V((peers, 8, rows), F32)]
        + [dma((4,)), dma((4,)), dma((4,)), dma((4,)), dma((2 * reach,)), dma((2 * reach,)), dma((peers,)), dma((peers,))]
    )
    out = jax.ShapeDtypeStruct((rows, width), BF)
    anywhere = pl.BlockSpec(memory_space=pl.ANY)
    return pl.pallas_call(
        functools.partial(kernel, heads, blocks, head_devs, reach),
        out_shape=[out] * 4,
        in_specs=[anywhere] * 4
        + [pl.BlockSpec(memory_space=pltpu.VMEM), pl.BlockSpec(memory_space=pltpu.SMEM)],
        out_specs=[anywhere] * 4,
        scratch_shapes=scratch,
        compiler_params=pltpu.CompilerParams(
            collective_id=0, has_side_effects=True, vmem_limit_bytes=56 * 1024 * 1024
        ),
    )(queries, key_vectors, value_vectors, out_grad, segment_ids.reshape(1, rows), head_gain)


def solution(mesh):
    wide = P("ctx", "head")
    return jax.shard_map(
        per_device,
        mesh=mesh,
        in_specs=(wide, wide, wide, wide, P("ctx"), P("head")),
        out_specs=(wide, wide, wide, wide),
        check_vma=False,
    )
```

```python
import functools

import jax
import jax.numpy as jnp
from jax import lax
from jax.experimental import pallas as pl
from jax.experimental.pallas import tpu as pltpu
from jax.sharding import PartitionSpec as P

HS = 128
EPS = 1e-05
CHUNK = 256
BF = jnp.bfloat16
F32 = jnp.float32


def dot(a, b, da, db):
    return lax.dot_general(a, b, (((da,), (db,)), ((), ())), preferred_element_type=F32)


def kernel(
    heads, blocks, head_devs, reach,
    q_hbm, k_hbm, v_hbm, g_hbm, seg_ref, gain_ref,
    att_hbm, gq_hbm, gkl_hbm, gvl_hbm, close_out, grad_out,
    q, k, v, g, att, gq,
    scaled, inner, gkl, gvl, probs, masks, segc,
    use_f, use_b, in_chunk_close, in_chunk_open, in_open, in_close,
    rr, xc, accp, accx, states, ustates, state_in, state_grad,
    tail_f, got_f, comb_f, far_f, back_f, home_f,
    tail_b, got_b, comb_b, far_b, back_b, home_b,
    pc_send, pc_recv,
    load_sem, kv_sem, store_sem, part_sem, pair_send, pair_recv, far_send, far_recv, pc_ssem, pc_rsem,
):
    rows = q.shape[0]
    chunks = rows // CHUNK
    half = heads // 2
    hr = half * HS
    pairs = blocks // 2
    me = lax.axis_index("ctx")
    hd = lax.axis_index("head")
    pair = me // 2
    core = me % 2
    partner = pair * 2 + 1 - core

    loads = [
        pltpu.make_async_copy(s, d, load_sem.at[i])
        for i, (s, d) in enumerate(((q_hbm, q), (g_hbm, g)))
    ]

    def cols(h):
        return pl.ds(pl.multiple_of(h * HS, HS), HS)

    def kv_load(h):
        return [
            pltpu.make_async_copy(s.at[:, cols(h)], d.at[:, cols(h)], kv_sem.at[i, h])
            for i, (s, d) in enumerate(((k_hbm, k), (v_hbm, v)))
        ]

    def start_kv(h, _):
        for cp in kv_load(h):
            cp.start()
        return 0

    lax.fori_loop(0, heads, start_kv, 0)
    for cp in loads:
        cp.start()

    barrier = pltpu.get_barrier_semaphore()
    pl.semaphore_signal(barrier, inc=1, device_id={"ctx": partner}, device_id_type=pl.DeviceIdType.MESH)
    count = jnp.int32(1)
    for r in range(1, reach + 1):
        for sign in (1, -1):
            other = pair + sign * r
            ok = (other >= 0) & (other < pairs)
            count = count + ok.astype(jnp.int32)

            @pl.when(ok)
            def _(other=other):
                pl.semaphore_signal(
                    barrier, inc=1, device_id={"ctx": other * 2 + core}, device_id_type=pl.DeviceIdType.MESH
                )
    for d in range(1, head_devs):
        pl.semaphore_signal(
            barrier, inc=1, device_id={"head": (hd + d) % head_devs}, device_id_type=pl.DeviceIdType.MESH
        )
        count = count + 1

    seg_row = seg_ref[...].astype(F32)
    segc[...] = jnp.broadcast_to(seg_row, (HS, rows)).T
    opens = [segc[pl.ds(j * CHUNK, 1), :] for j in range(chunks)]
    closes = [segc[pl.ds(j * CHUNK + CHUNK - 1, 1), :] for j in range(chunks)]
    own_open, own_close = opens[0], closes[-1]

    def same(a, b):
        return jnp.where(a == b, 1.0, 0.0)

    causal = lax.broadcasted_iota(jnp.int32, (CHUNK, CHUNK), 0) >= lax.broadcasted_iota(
        jnp.int32, (CHUNK, CHUNK), 1
    )
    for j in range(chunks):
        at = pl.ds(j * CHUNK, CHUNK)
        s = segc[at, :]
        in_chunk_close[at, :] = same(s, closes[j]).astype(BF)
        in_chunk_open[at, :] = same(s, opens[j]).astype(BF)
        in_open[at, :] = same(s, own_open).astype(BF)
        in_close[at, :] = same(s, own_close).astype(BF)
        use_f[at, :] = same(s, closes[max(j - 1, 0)]).astype(BF)
        use_b[at, :] = same(s, opens[min(j + 1, chunks - 1)]).astype(BF)
        wide = jnp.concatenate([s] * (CHUNK // HS), axis=1)
        row = seg_ref[:, j * CHUNK : (j + 1) * CHUNK].astype(F32)
        masks[j] = jnp.where(causal & (wide == row), 1.0, 0.0)
    pass_f = [None] + [same(closes[j], closes[j - 1]) for j in range(1, chunks)]
    pass_b = [same(opens[j], opens[j + 1]) for j in range(chunks - 1)] + [None]

    line = lax.broadcasted_iota(jnp.int32, (8, HS), 0)
    marks = jnp.where(line == 0, own_open, own_close)
    for share in range(2):
        tail_f[share, pl.ds(hr, 8), :] = marks
        tail_b[share, pl.ds(hr, 8), :] = marks

    def each_head(start, stop, body):
        def turn(h, _):
            body(h, cols(h))
            return 0

        lax.fori_loop(start, stop, turn, 0, unroll=2 if (stop - start) % 2 == 0 else 1)

    class Exchange:
        def __init__(self, way, tail, got, comb, far, back, home, result):
            self.way, self.base = way, 0 if way > 0 else 1
            self.tail, self.got, self.comb, self.far = tail, got, comb, far
            self.back, self.home, self.result = back, home, result
            self.first = core == (0 if way > 0 else 1)
            i = self.base * 2
            self.out = pltpu.make_async_remote_copy(
                src_ref=tail.at[1 - core], dst_ref=got,
                send_sem=pair_send.at[i], recv_sem=pair_recv.at[i],
                device_id={"ctx": partner}, device_id_type=pl.DeviceIdType.MESH,
            )
            self.ret = pltpu.make_async_remote_copy(
                src_ref=back, dst_ref=home,
                send_sem=pair_send.at[i + 1], recv_sem=pair_recv.at[i + 1],
                device_id={"ctx": partner}, device_id_type=pl.DeviceIdType.MESH,
            )

        def hop(self, r):
            i = self.base * reach + r - 1
            return pltpu.make_async_remote_copy(
                src_ref=self.comb, dst_ref=self.far.at[r - 1],
                send_sem=far_send.at[i], recv_sem=far_recv.at[i],
                device_id={"ctx": (pair + self.way * r) * 2 + core},
                device_id_type=pl.DeviceIdType.MESH,
            )

        def inside(self, r):
            other = pair + r
            return (other >= 0) & (other < pairs)

        def both(self):
            other_open = self.got[pl.ds(hr, 1), :]
            other_close = self.got[pl.ds(hr + 1, 1), :]
            if self.way > 0:
                own, oth = (own_close, own_open), (other_close, other_open)
            else:
                own, oth = (own_open, own_close), (other_open, other_close)
            pick = [(jnp.where(self.first, a, b), jnp.where(self.first, b, a)) for a, b in zip(own, oth)]
            return pick

        def middle(self):
            self.out.wait()
            (tag_first, tag_last), _ = self.both()
            joined = tag_first == tag_last

            def turn(e, _):
                at = pl.ds(pl.multiple_of(e * HS, HS), HS)
                mine, other = self.tail[core, at, :], self.got[at, :]
                t_first = jnp.where(self.first, mine, other)
                t_last = jnp.where(self.first, other, mine)
                self.comb[at, :] = t_last + jnp.where(joined, t_first, 0.0)
                return 0

            lax.fori_loop(0, half, turn, 0)
            self.comb[pl.ds(hr, 8), :] = jnp.broadcast_to(tag_last, (8, HS))
            for r in range(1, reach + 1):

                @pl.when(self.inside(self.way * r))
                def _(r=r):
                    self.hop(r).start()

                @pl.when(jnp.logical_not(self.inside(-self.way * r)))
                def _(r=r):
                    self.far[r - 1] = jnp.full((hr + 8, HS), -1.0, F32)

        def near(self):
            for r in range(1, reach + 1):

                @pl.when(self.inside(-self.way * r))
                def _(r=r):
                    self.hop(r).wait_recv()

            (tag_first, _), (need_first, need_last) = self.both()
            tags = [self.far[r, pl.ds(hr, 1), :] for r in range(reach)]

            def turn(e, _):
                at = pl.ds(pl.multiple_of(e * HS, HS), HS)
                t_first = jnp.where(self.first, self.tail[core, at, :], self.got[at, :])
                x_first = jnp.zeros((HS, HS), F32)
                x_last = jnp.where(tag_first == need_last, t_first, 0.0)
                for r in range(reach):
                    c = self.far[r, at, :]
                    x_first = x_first + jnp.where(tags[r] == need_first, c, 0.0)
                    x_last = x_last + jnp.where(tags[r] == need_last, c, 0.0)
                self.back[at, :] = jnp.where(self.first, x_last, x_first)
                self.result[core * half + e] = jnp.where(self.first, x_first, x_last).astype(BF)
                return 0

            lax.fori_loop(0, half, turn, 0)
            self.ret.start()

        def finish(self):
            self.ret.wait()

            def turn(e, _):
                at = pl.ds(pl.multiple_of(e * HS, HS), HS)
                self.result[(1 - core) * half + e] = self.home[at, :].astype(BF)
                return 0

            lax.fori_loop(0, half, turn, 0)
            for r in range(1, reach + 1):

                @pl.when(self.inside(self.way * r))
                def _(r=r):
                    self.hop(r).wait_send()

    fwd = Exchange(1, tail_f, got_f, comb_f, far_f, back_f, home_f, state_in)
    bwd = Exchange(-1, tail_b, got_b, comb_b, far_b, back_b, home_b, state_grad)

    def tails(h, c):
        for cp in kv_load(h):
            cp.wait()
        s = None
        for j in range(chunks):
            at = pl.ds(j * CHUNK, CHUNK)
            t = dot(k[at, c] * in_chunk_close[at, :], v[at, c], 0, 0)
            s = t if j == 0 else s * pass_f[j] + t
            if j < chunks - 1:
                states[h, j] = s.astype(BF)
        tail_f[h // half, pl.ds(pl.multiple_of((h % half) * HS, HS), HS), :] = s

    each_head(0, heads, tails)
    pl.semaphore_wait(barrier, count)
    fwd.out.start()
    loads[0].wait()

    def local(h, c):
        for j in range(chunks):
            at = pl.ds(j * CHUNK, CHUNK)
            qj = q[at, c]
            p = (dot(qj, k[at, c], 1, 1) * masks[j]).astype(BF)
            probs[h, j] = p
            o = dot(p, v[at, c], 1, 0)
            if j > 0:
                o = o + dot(qj * use_f[at, :], states[h, j - 1], 1, 0)
            scaled[at, c] = o

    early = max(1, heads // 4)
    each_head(0, early, local)
    fwd.middle()
    each_head(early, heads, local)
    loads[1].wait()
    fwd.near()
    accp[...] = jnp.zeros_like(accp)
    accx[...] = jnp.zeros_like(accx)
    fwd.finish()

    def norm(h, c):
        gain = gain_ref[h]
        for j in range(chunks):
            at = pl.ds(j * CHUNK, CHUNK)
            a = scaled[at, c] + dot(q[at, c] * in_open[at, :], state_in[h], 1, 0)
            a = a * gain
            scaled[at, c] = a
            accp[at, :] += a * a
            accx[at, :] += a * g[at, c].astype(F32)

    each_head(0, heads, norm)

    pc_send[pl.ds(0, 1), :] = jnp.sum(accp[...].T, axis=0, keepdims=True)
    pc_send[pl.ds(1, 1), :] = jnp.sum(accx[...].T, axis=0, keepdims=True)
    pc_send[pl.ds(2, 6), :] = jnp.zeros((6, rows), F32)
    swaps = [
        pltpu.make_async_remote_copy(
            src_ref=pc_send, dst_ref=pc_recv.at[d - 1],
            send_sem=pc_ssem.at[d - 1], recv_sem=pc_rsem.at[d - 1],
            device_id={"head": (hd + d) % head_devs}, device_id_type=pl.DeviceIdType.MESH,
        )
        for d in range(1, head_devs)
    ]
    for cp in swaps:
        cp.start()
    for cp in swaps:
        cp.wait()
    power, cross = pc_send[pl.ds(0, 1), :], pc_send[pl.ds(1, 1), :]
    for d in range(head_devs - 1):
        power = power + pc_recv[d, pl.ds(0, 1), :]
        cross = cross + pc_recv[d, pl.ds(1, 1), :]
    width = head_devs * heads * HS
    r = lax.rsqrt(power / width + EPS)
    rr[...] = jnp.broadcast_to(r, (HS, rows)).T
    xc[...] = jnp.broadcast_to(cross * r * r * r / width, (HS, rows)).T

    def inners(h, c):
        gain = gain_ref[h]
        u = None
        for j in reversed(range(chunks)):
            at = pl.ds(j * CHUNK, CHUNK)
            a, rj = scaled[at, c], rr[at, :]
            att[at, c] = (a * rj).astype(BF)
            i = (gain * (g[at, c].astype(F32) * rj - a * xc[at, :])).astype(BF)
            inner[at, c] = i
            b = dot(q[at, c] * in_chunk_open[at, :], i, 0, 0)
            u = b if j == chunks - 1 else u * pass_b[j] + b
            if j > 0:
                ustates[h, j - 1] = u.astype(BF)
        tail_b[h // half, pl.ds(pl.multiple_of((h % half) * HS, HS), HS), :] = u

    each_head(0, heads, inners)
    bwd.out.start()
    stores = [
        pltpu.make_async_copy(s, d, store_sem.at[i])
        for i, (s, d) in enumerate(((att, att_hbm), (gq, gq_hbm)))
    ]
    stores[0].start()

    def parts(h):
        return [
            pltpu.make_async_copy(s.at[:, cols(h)], d.at[:, cols(h)], part_sem.at[i, h])
            for i, (s, d) in enumerate(((gkl, gkl_hbm), (gvl, gvl_hbm)))
        ]

    def grads(h, c):
        for j in range(chunks):
            at = pl.ds(j * CHUNK, CHUNK)
            i, kj, vj = inner[at, c], k[at, c], v[at, c]
            d = (dot(i, vj, 1, 1) * masks[j]).astype(BF)
            a = dot(d, kj, 1, 0) + dot(i * in_open[at, :], state_in[h], 1, 1)
            if j > 0:
                a = a + dot(i * use_f[at, :], states[h, j - 1], 1, 1)
            gq[at, c] = a.astype(BF)
            b = dot(d, q[at, c], 0, 0)
            e = dot(probs[h, j], i, 0, 0)
            if j < chunks - 1:
                b = b + dot(vj * use_b[at, :], ustates[h, j], 1, 1)
                e = e + dot(kj * use_b[at, :], ustates[h, j], 1, 0)
            gkl[at, c] = b
            gvl[at, c] = e
        for cp in parts(h):
            cp.start()

    each_head(0, early, grads)
    bwd.middle()
    each_head(early, heads, grads)
    stores[1].start()
    bwd.near()
    bwd.finish()

    close_out[...] = in_close[...]
    grad_out[...] = state_grad[...]

    def drain(h, _):
        for cp in parts(h):
            cp.wait()
        return 0

    lax.fori_loop(0, heads, drain, 0)
    for cp in stores:
        cp.wait()


def finish_kernel(heads, att, gq, gkl, gvl, k, v, close, grad, att_out, gq_out, gk_out, gv_out):
    att_out[...] = att[...]
    gq_out[...] = gq[...]
    m = close[...]
    for h in range(heads):
        c = slice(h * HS, (h + 1) * HS)
        gk_out[:, c] = (gkl[:, c] + dot(v[:, c] * m, grad[h], 1, 1)).astype(BF)
        gv_out[:, c] = (gvl[:, c] + dot(k[:, c] * m, grad[h], 1, 0)).astype(BF)


def per_device(queries, key_vectors, value_vectors, out_grad, segment_ids, head_gain):
    rows, width = queries.shape
    heads = head_gain.shape[0]
    blocks = lax.axis_size("ctx")
    head_devs = lax.axis_size("head")
    reach = max(1, (blocks // 4 + 1) // 2)
    chunks = rows // CHUNK
    hr = heads // 2 * HS
    V = pltpu.VMEM
    whole = V((rows, width), BF)
    lanes = V((rows, HS), BF)
    flanes = V((rows, HS), F32)
    msg = V((hr + 8, HS), F32)
    comm = [V((2, hr + 8, HS), F32), msg, msg, V((reach, hr + 8, HS), F32), V((hr, HS), F32), V((hr, HS), F32)]
    peers = max(1, head_devs - 1)
    dma = pltpu.SemaphoreType.DMA
    scratch = (
        [whole] * 6
        + [V((rows, width), F32), whole, V((rows, width), F32), V((rows, width), F32)]
        + [V((heads, chunks, CHUNK, CHUNK), BF), V((chunks, CHUNK, CHUNK), F32), flanes]
        + [lanes] * 6
        + [flanes] * 4
        + [V((heads, chunks - 1, HS, HS), BF)] * 2
        + [V((heads, HS, HS), BF)] * 2
        + comm
        + comm
        + [V((8, rows), F32), V((peers, 8, rows), F32)]
        + [dma((2,)), dma((2, heads)), dma((2,)), dma((2, heads)), dma((4,)), dma((4,)), dma((2 * reach,)), dma((2 * reach,)), dma((peers,)), dma((peers,))]
    )
    out = jax.ShapeDtypeStruct((rows, width), BF)
    anywhere = pl.BlockSpec(memory_space=pl.ANY)
    part = jax.ShapeDtypeStruct((rows, width), F32)
    att, gq, gkl, gvl, close, grad = pl.pallas_call(
        functools.partial(kernel, heads, blocks, head_devs, reach),
        out_shape=[out, out, part, part, jax.ShapeDtypeStruct((rows, HS), BF), jax.ShapeDtypeStruct((heads, HS, HS), BF)],
        in_specs=[anywhere] * 4
        + [pl.BlockSpec(memory_space=pltpu.VMEM), pl.BlockSpec(memory_space=pltpu.SMEM)],
        out_specs=[anywhere] * 4 + [pl.BlockSpec(memory_space=pltpu.VMEM)] * 2,
        scratch_shapes=scratch,
        compiler_params=pltpu.CompilerParams(
            collective_id=0, has_side_effects=True, vmem_limit_bytes=56 * 1024 * 1024
        ),
    )(queries, key_vectors, value_vectors, out_grad, segment_ids.reshape(1, rows), head_gain)
    step = 128
    wide = pl.BlockSpec((step, width), lambda i: (i, 0))
    return pl.pallas_call(
        functools.partial(finish_kernel, heads),
        grid=(rows // step,),
        out_shape=[out] * 4,
        in_specs=[wide] * 6
        + [pl.BlockSpec((step, HS), lambda i: (i, 0)), pl.BlockSpec((heads, HS, HS), lambda i: (0, 0, 0))],
        out_specs=[wide] * 4,
        compiler_params=pltpu.CompilerParams(vmem_limit_bytes=56 * 1024 * 1024),
    )(att, gq, gkl, gvl, key_vectors, value_vectors, close, grad)


def solution(mesh):
    wide = P("ctx", "head")
    return jax.shard_map(
        per_device,
        mesh=mesh,
        in_specs=(wide, wide, wide, wide, P("ctx"), P("head")),
        out_specs=(wide, wide, wide, wide),
        check_vma=False,
    )
```
